32 devices in a mesh: sub: 16 (over z, y, x), rhs: 2 (over core).
Axes of the slice: x: 2, y: 2, z: 4, core: 2. Of those that a mesh axis runs over, the one named last changes fastest.
Arguments:
- schur_block: bfloat16 [32, 1024, 1024], P('sub', 'rhs'), may hold values from -1 to 4, as said below
- scaling: float32 [32, 1024], P('sub'), may hold values from 0.25 to 1.75
- gravity_load: float32 [32, 1024, 256], P('sub', None, 'rhs'), may hold values from -100 to 100
- pressure: bfloat16 [1024, 4, 256], P('sub', None, 'rhs'), may hold values from -6 to 6
- block_target: int32 [1024, 1], P('sub'), may hold values from 0 to 31; in each aligned block of 64 rows (0 to 63, 64 to 127, ...) at most 4 rows name the same one
- aero_interp: float32 [4, 1024], replicated, may hold values from -0.5 to 0.5
- partner_slot: int32 [4, 32], P(None, 'sub'), may hold values from 0 to 1, as said below
- corner_row: int32 [32, 8], P('sub'), may hold values from 0 to 1023
- corner_coarse: int32 [32, 8], P('sub'), may hold values from 0 to 127
- coarse_inverse: float32 [128, 128], P('sub'), may hold values from -1 to 6, as said below
Outputs:
- solution: float32 [32, 1024, 256], P('sub', None, 'rhs')
The draws below stay inside these ranges and needn't reach their ends.
Inputs may be any that keep to these rules, and one draw needn't show every extreme that they name: `block_target`: at most 4 of the blocks of one device name the same subdomain; in some device's blocks one subdomain is named exactly 4 times; every subdomain is named by some block. In round k, subdomain s on device d = s // 2 is paired with subdomain (d xor 2^k) * 2 + partner_slot[k, s]; the pairing is mutual. `schur_block`: each matrix is symmetric. `coarse_inverse`: symmetric.
All inputs are finite; a program needn't handle non-finite values.
Results may differ from the reference program's by a relative error of at most 0.0027.
Values may be sent and summed in bfloat16 or wider, within the bound.
A program may use at most 64 MiB of HBM per device.

```python
import math
import jax
import jax.numpy as jnp
import numpy as np
from jax import lax

SUB_DEV = 2
M = 1024
FACES = 4
PB = 4
MOST = 4
NC = 8
ITERS = 2
NSUB = 32
FW = 256
RHS = 256
BLK_DEV = 64
BLOCKS = 1024
NCO = 128
N_SUB = 16


def draw_schur_block(key, part):
    identity = jnp.arange(M)[:, None] == jnp.arange(M)[None, :]
    off_scale = 0.7 / M ** 0.5

    def draw_one(sub_index):
        sub_key = jax.random.fold_in(key, sub_index)
        offdiag = jax.random.uniform(sub_key, (M, M), jnp.float32, -1.0, 1.0)
        offdiag = (offdiag + offdiag.T) * off_scale
        diagonal = jax.random.uniform(jax.random.fold_in(sub_key, 1), (M,), jnp.float32, 2.0, 3.5)
        return jnp.where(identity, diagonal[:, None], offdiag).astype(jnp.bfloat16)
    return lax.map(draw_one, jnp.arange(NSUB))


def draw_coarse_inverse(key, part):
    identity = jnp.arange(NCO)[:, None] == jnp.arange(NCO)[None, :]
    off_scale = 1.1 / NCO ** 0.5
    offdiag = jax.random.uniform(key, (NCO, NCO), jnp.float32, -1.0, 1.0)
    offdiag = (offdiag + offdiag.T) * off_scale
    diagonal = jax.random.uniform(jax.random.fold_in(key, 1), (NCO,), jnp.float32, 3.0, 6.0)
    return jnp.where(identity, diagonal[:, None], offdiag)


def draw_gravity_load(key, part):
    position = jnp.arange(NSUB, dtype=jnp.float32)
    rise_factor = 0.5 + 1.5 * position / max(NSUB - 1, 1)
    base_field = jax.random.normal(key, (NSUB, M, RHS), jnp.float32)
    return base_field * rise_factor[:, None, None]


def draw_partner_slot(key, part):
    device_count = NSUB // SUB_DEV
    device_id = jnp.arange(device_count, dtype=jnp.int32)
    slot_rows = []
    for face_index in range(FACES):
        scores = jax.random.randint(jax.random.fold_in(key, face_index), (device_count, SUB_DEV), 0, 1 << 20)
        scores = scores * SUB_DEV + jnp.arange(SUB_DEV, dtype=jnp.int32)[None, :]
        forward = jnp.argsort(scores, axis=1).astype(jnp.int32)
        inverse = jnp.argsort(forward, axis=1).astype(jnp.int32)
        bit_value = 2 ** face_index
        upper = device_id // bit_value % 2 == 1
        lower = jnp.where(upper, device_id - bit_value, device_id)
        slot_row = jnp.where(upper[:, None], inverse[lower], forward[lower])
        slot_rows.append(slot_row.reshape(-1))
    return jnp.stack(slot_rows).astype(jnp.int32)


def set_ends(entries, key, smallest, largest):
    extent = entries.shape
    place = [jax.random.randint(jax.random.fold_in(key, axis), (), 0, extent[axis]) for axis in range(len(extent))]
    entries = entries.at[tuple(place)].set(smallest)
    longest = extent.index(max(extent))
    place[longest] = (place[longest] + 1) % extent[longest]
    return entries.at[tuple(place)].set(largest)


def steps_of(key, dims, shards, smallest, largest):
    level = 1.0
    for dim, parts in shards:
        draws = jax.random.uniform(jax.random.fold_in(jax.random.fold_in(key, 6), dim), (parts,), jnp.float32, smallest / len(shards), largest / len(shards))
        level = level * jnp.repeat(jnp.exp(draws), dims[dim] // parts).reshape((-1,) + (1,) * (len(dims) - 1 - dim))
    return level


def shared_out(key, own, number, rows, number_of, top, most, lean):
    sequence = jax.random.permutation(key, number_of)
    packed, common = load_shares(number_of, rows * top, most, lean, True), load_shares(number_of, rows * top, most, lean, False)
    places = jnp.arange(number_of)

    def named(tallies, rotation):
        used = int((tallies > 0).sum())
        fixed = max(1, used // 4)
        passed = fixed + (places - fixed + rotation * (used - fixed)) % max(1, number_of - fixed)
        return jnp.zeros((number_of,), jnp.int32).at[sequence[jnp.where(places < fixed, places, passed)]].set(jnp.asarray(tallies, jnp.int32))

    tallies = jnp.where(number % 4 == 0, named(packed, number // 4), named(common, number - number // 4 - 1))
    mixed = jax.random.permutation(jax.random.fold_in(own, 3), number_of)
    giver, taker = mixed[0:number_of // 2 * 2:2], mixed[1:number_of // 2 * 2:2]
    slack = jnp.minimum(tallies[giver] - 1, most - tallies[taker]) // 2
    slack = jnp.where((giver == sequence[0]) | (taker == sequence[0]) | (tallies[taker] == 0), 0, jnp.maximum(slack, 0))
    passed = jax.random.randint(jax.random.fold_in(own, 4), (number_of // 2,), 0, 1 << 20) % (slack + 1)
    tallies = tallies.at[giver].add(-passed).at[taker].add(passed)
    labels = jnp.searchsorted(jnp.cumsum(tallies), jnp.arange(rows * top), side="right").astype(jnp.int32)
    listing = labels.reshape(top, rows).T
    listing = listing[jax.random.permutation(jax.random.fold_in(own, 1), rows)]
    rotation = jax.random.randint(jax.random.fold_in(own, 2), (rows, 1), 0, top)
    return jnp.take_along_axis(listing, (jnp.arange(top)[None, :] + rotation) % top, axis=1)


def load_shares(amount, total, reach, skew, full):
    portions = [(1 << 20) // math.isqrt(standing ** skew) + 1 for standing in range(1, amount + 1)]
    largest = reach if full else min(reach, max(-(-total // amount), total * portions[0] // sum(portions)))
    least = 1 if total - largest >= amount - 1 else 0
    counts, rest = [largest] + [least] * (amount - 1), total - largest - least * (amount - 1)
    while rest > 0:
        movable = [i for i in range(1, amount) if counts[i] < largest] or [i for i in range(1, amount) if counts[i] < reach]
        whole, left = sum([portions[i] for i in movable]), rest
        for i in movable:
            addition = min(reach - counts[i], max(1, left * portions[i] // whole), rest)
            counts[i] = counts[i] + addition
            rest = rest - addition
    return np.array(counts)


def bell_draw(key, extent, width, bound, pieces=(), kind=jnp.bfloat16):
    result = width * jax.random.normal(key, extent, jnp.float32)
    if pieces:
        result = result * steps_of(key, extent, pieces, -0.22, 0.18)
    return jnp.clip(result, -bound, bound).astype(kind)


def setup_inputs(seed: int = 0) -> dict:
    seeds = jax.random.split(jax.random.key(seed), 11)
    schur_block = draw_schur_block(jax.random.fold_in(seeds[10], 71), 0)
    scaling = jnp.clip(1.0 + 0.15 * jax.random.normal(seeds[1], (NSUB, M), jnp.float32), 0.25, 1.75)
    gravity_load = draw_gravity_load(jax.random.fold_in(seeds[10], 71), 0)
    pressure = bell_draw(seeds[3], (BLOCKS, PB, RHS), 1.0, 6.0, ((0, 16), (2, 2)))
    block_target_keys = jax.random.split(jax.random.fold_in(seeds[4], 1), BLOCKS // BLK_DEV)
    block_target_turns = jax.random.permutation(jax.random.fold_in(seeds[4], 3), BLOCKS // BLK_DEV)
    block_target = jax.vmap(lambda own, number: shared_out(jax.random.fold_in(seeds[4], 2), own, number, BLK_DEV, NSUB, 1, MOST, 2))(block_target_keys, block_target_turns).reshape((BLOCKS, 1))
    aero_interp = bell_draw(seeds[5], (PB, M), (2 * PB * N_SUB) ** -0.5, 0.5, (), jnp.float32)
    partner_slot = draw_partner_slot(jax.random.fold_in(seeds[10], 71), 0)
    corner_row = set_ends(jax.random.randint(seeds[7], (NSUB, NC), 0, M), jax.random.fold_in(seeds[7], 1), 0, M - 1).astype(jnp.int32)
    corner_coarse = set_ends(jax.random.randint(seeds[8], (NSUB, NC), 0, NCO), jax.random.fold_in(seeds[8], 1), 0, NCO - 1).astype(jnp.int32)
    coarse_inverse = draw_coarse_inverse(jax.random.fold_in(seeds[10], 71), 0)
    return dict(schur_block=schur_block, scaling=scaling, gravity_load=gravity_load, pressure=pressure, block_target=block_target, aero_interp=aero_interp, partner_slot=partner_slot, corner_row=corner_row, corner_coarse=corner_coarse, coarse_inverse=coarse_inverse)


coupling = 2.0


def schur_apply(schur_block, rounded):
    group_count = NSUB // SUB_DEV
    matrices = schur_block.reshape(group_count, SUB_DEV, M, M)
    vectors = rounded.reshape(group_count, SUB_DEV, M, RHS)

    def apply_group(pair):
        return jnp.einsum("snm,smc->snc", pair[0].astype(jnp.float32), pair[1].astype(jnp.float32), precision=lax.Precision.HIGHEST)

    return lax.map(apply_group, (matrices, vectors)).reshape(NSUB, M, RHS)


def jump_terms(rounded, partner_slot):
    values = rounded.astype(jnp.float32)
    device_id = jnp.arange(NSUB, dtype=jnp.int32) // SUB_DEV
    face_terms = []
    for face_index in range(FACES):
        bit_value = 2 ** face_index
        upper = (device_id // bit_value) % 2
        partner = (device_id + bit_value - 2 * bit_value * upper) * SUB_DEV + partner_slot[face_index]
        own_face = values[:, face_index * FW:(face_index + 1) * FW, :]
        face_terms.append(coupling * (own_face - own_face[partner]))
    return jnp.concatenate(face_terms, axis=1)


def operator(direction, schur_block, partner_slot):
    rounded = direction.astype(jnp.bfloat16)
    return schur_apply(schur_block, rounded) + jump_terms(rounded, partner_slot)


def precondition(residual, schur_block, scaling, corner_row, corner_coarse, coarse_inverse):
    weight_col = scaling[:, :, None]
    dirichlet = weight_col * schur_apply(schur_block, (weight_col * residual).astype(jnp.bfloat16))
    sub_rows = jnp.arange(NSUB, dtype=jnp.int32)[:, None]
    picked = residual[sub_rows, corner_row]
    coarse = jnp.zeros((NCO, RHS), jnp.float32).at[corner_coarse.reshape(-1)].add(picked.reshape(-1, RHS))
    solved = jnp.dot(coarse_inverse, coarse, precision=lax.Precision.HIGHEST)
    corner_add = jnp.zeros_like(residual).at[sub_rows, corner_row].add(solved[corner_coarse])
    return dirichlet + corner_add


def reference(schur_block, scaling, gravity_load, pressure, block_target, aero_interp, partner_slot, corner_row, corner_coarse, coarse_inverse):
    load_sum = jnp.zeros((NSUB, PB, RHS), jnp.float32).at[block_target[:, 0]].add(pressure.astype(jnp.float32))
    force_total = gravity_load + jnp.einsum("pm,spc->smc", aero_interp, load_sum, precision=lax.Precision.HIGHEST)
    solution = jnp.zeros_like(force_total)
    residual = force_total
    precond = precondition(residual, schur_block, scaling, corner_row, corner_coarse, coarse_inverse)
    direction = precond
    precond_dot = jnp.sum(residual * precond, axis=(0, 1))
    for step_index in range(ITERS):
        applied = operator(direction, schur_block, partner_slot)
        step_size = precond_dot / jnp.sum(direction * applied, axis=(0, 1))
        solution = solution + step_size * direction
        residual = residual - step_size * applied
        if step_index + 1 < ITERS:
            precond = precondition(residual, schur_block, scaling, corner_row, corner_coarse, coarse_inverse)
            next_product = jnp.sum(residual * precond, axis=(0, 1))
            direction = precond + (next_product / precond_dot) * direction
            precond_dot = next_product
    return solution
```

```python
import jax
import jax.numpy as jnp
from jax import lax
from jax.sharding import PartitionSpec as P

SUB_DEV = 2
FACES = 4
MOST = 4
ITERS = 2
FW = 256


coupling = 2.0


def swapped(shard, axis, distance):
    return lax.ppermute(shard, axis, [(i, i ^ 1 << distance) for i in range(lax.axis_size(axis))])


def all_sum(value):
    distance = 0
    while 1 << distance < lax.axis_size("sub"):
        value = value + swapped(value, "sub", distance)
        distance += 1
    return value


def schur_apply(schur_block, rounded):
    half_rows = jnp.einsum(
        "snm,smc->snc",
        schur_block,
        lax.all_gather(rounded, "rhs", axis=2, tiled=True),
        preferred_element_type=jnp.float32,
    )
    return lax.all_to_all(half_rows, "rhs", split_axis=2, concat_axis=1, tiled=True)


def jump_terms(rounded, partner_slot):
    face_terms = []
    for face_index in range(FACES):
        own_face = rounded[:, face_index * FW : (face_index + 1) * FW, :]
        partner_face = swapped(own_face, "sub", face_index)
        select = (
            partner_slot[face_index][:, None] == jnp.arange(SUB_DEV, dtype=jnp.int32)[None, :]
        ).astype(jnp.bfloat16)
        picked = jnp.einsum("sj,jfc->sfc", select, partner_face, preferred_element_type=jnp.float32)
        face_terms.append(coupling * (own_face.astype(jnp.float32) - picked))
    return jnp.concatenate(face_terms, axis=1)


def operator(direction, schur_block, partner_slot):
    rounded = direction.astype(jnp.bfloat16)
    return schur_apply(schur_block, rounded) + jump_terms(rounded, partner_slot)


def coarse_solve(coarse, coarse_inverse):
    own_rows = jnp.dot(coarse_inverse, coarse, precision=lax.Precision.HIGHEST)
    start = lax.axis_index("sub") * own_rows.shape[0]
    whole = jnp.zeros_like(coarse)
    return all_sum(lax.dynamic_update_slice(whole, own_rows, (start, 0)))


def add_corners(solved, corner_row, corner_coarse, residual):
    sub_rows = jnp.arange(SUB_DEV, dtype=jnp.int32)[:, None]
    return jnp.zeros_like(residual).at[sub_rows, corner_row].add(solved[corner_coarse])


def precondition(residual, schur_block, scaling, corner_row, corner_coarse, coarse_inverse):
    columns = residual.shape[2]
    weight_col = scaling[:, :, None]
    dirichlet = weight_col * schur_apply(schur_block, (weight_col * residual).astype(jnp.bfloat16))
    sub_rows = jnp.arange(SUB_DEV, dtype=jnp.int32)[:, None]
    picked = residual[sub_rows, corner_row]
    partial_sum = (
        jnp.zeros((coarse_inverse.shape[1], columns), jnp.float32)
        .at[corner_coarse.reshape(-1)]
        .add(picked.reshape(-1, columns))
    )
    coarse = all_sum(partial_sum)
    solved = coarse_solve(coarse, coarse_inverse)
    precond = dirichlet + add_corners(solved, corner_row, corner_coarse, residual)
    product_value = all_sum(jnp.sum(residual * precond, axis=(0, 1)))
    return (precond, product_value)


def on_device(
    schur_block,
    scaling,
    gravity_load,
    pressure,
    block_target,
    aero_interp,
    partner_slot,
    corner_row,
    corner_coarse,
    coarse_inverse,
):
    sub_count = lax.axis_size("sub")
    all_subdomains = SUB_DEV * sub_count
    columns = gravity_load.shape[2]
    points = pressure.shape[1]
    target = block_target[:, 0]
    matches = target[:, None] == target[None, :]
    before = jnp.tril(matches, -1)
    rank_in = jnp.sum(before, axis=1, dtype=jnp.int32)
    slot_index = target * MOST + rank_in
    buffer = (
        jnp.zeros((all_subdomains * MOST, points, columns), jnp.bfloat16)
        .at[slot_index]
        .set(pressure)
    )
    arrived = lax.all_to_all(buffer, "sub", split_axis=0, concat_axis=0, tiled=True)
    load_sum = jnp.sum(
        arrived.reshape(sub_count, SUB_DEV, MOST, points, columns), axis=(0, 2), dtype=jnp.float32
    )
    force_total = gravity_load + jnp.einsum(
        "pm,spc->smc", aero_interp, load_sum, precision=lax.Precision.HIGHEST
    )
    solution = jnp.zeros_like(force_total)
    residual = force_total
    precond, precond_dot = precondition(
        residual, schur_block, scaling, corner_row, corner_coarse, coarse_inverse
    )
    direction = precond
    for step_index in range(ITERS):
        applied = operator(direction, schur_block, partner_slot)
        curvature = all_sum(jnp.sum(direction * applied, axis=(0, 1)))
        step_size = precond_dot / curvature
        solution = solution + step_size * direction
        residual = residual - step_size * applied
        if step_index + 1 < ITERS:
            precond, next_product = precondition(
                residual, schur_block, scaling, corner_row, corner_coarse, coarse_inverse
            )
            direction = precond + next_product / precond_dot * direction
            precond_dot = next_product
    return solution


def solution(mesh):
    return jax.shard_map(
        on_device,
        mesh=mesh,
        in_specs=(
            P("sub", "rhs", None),
            P("sub", None),
            P("sub", None, "rhs"),
            P("sub", None, "rhs"),
            P("sub", None),
            P(),
            P(None, "sub"),
            P("sub", None),
            P("sub", None),
            P("sub", None),
        ),
        out_specs=P("sub", None, "rhs"),
        check_vma=False,
    )
```

```python
import functools

import jax
import jax.numpy as jnp
from jax import lax
from jax.experimental import pallas as pl
from jax.experimental.pallas import tpu as pltpu
from jax.sharding import PartitionSpec as P

SUB_DEV = 2
FACES = 4
FW = 256
COUPLING = 2.0

MESH = pl.DeviceIdType.MESH
EXACT = lax.Precision.HIGHEST


def fold(value):
    return jnp.sum(value.reshape(-1, 8, value.shape[-1]), axis=0)


def kernel(
    n,
    chunks,
    schur,
    weight,
    gravity,
    loads,
    common,
    interp,
    spread,
    slots,
    corner_row,
    out,
    matrix,
    res,
    dirn,
    app,
    weighted,
    rounded,
    corner,
    mix,
    faces,
    picks_out,
    sums_out,
    dots_out,
    loads_in,
    common_in,
    picks_in,
    sums_in,
    dots_in,
    matrix_sem,
    face_send,
    face_recv,
    send_sem,
    recv_sem,
):
    me = lax.axis_index("sub")
    half = lax.axis_index("rhs")
    rows = schur.shape[1]
    corners = corner_row.shape[0] * corner_row.shape[1]
    per_sub = corner_row.shape[1]
    coarse_rows = common.shape[0] - corners
    blocks = gravity.shape[1] // FW
    half_blocks = rows // FW

    local = pltpu.make_async_copy(schur, matrix.at[half], matrix_sem.at[0])
    local.start()

    barrier = pltpu.get_barrier_semaphore()

    def greet(step, carry):
        pl.semaphore_signal(
            barrier, inc=1, device_id={"sub": lax.rem(me + step, n)}, device_id_type=MESH
        )
        return carry

    lax.fori_loop(1, n, greet, 0)
    pl.semaphore_signal(barrier, inc=1, device_id={"rhs": 1 - half}, device_id_type=MESH)
    pl.semaphore_wait(barrier, n)

    def send_all(which, source, target):
        def send(step, carry):
            peer = lax.rem(me + step, n)
            pltpu.make_async_remote_copy(
                src_ref=source(peer),
                dst_ref=target.at[me],
                send_sem=send_sem.at[which],
                recv_sem=recv_sem.at[which],
                device_id={"sub": peer},
                device_id_type=MESH,
            ).start()
            return carry

        lax.fori_loop(1, n, send, 0)
        target[me] = source(me)[...]

    def wait_all(sems, which, target):
        view = target.at[pl.ds(0, n - 1)]
        pltpu.make_async_copy(view, view, sems.at[which]).wait()

    send_all(0, lambda peer: loads.at[peer], loads_in)
    swap = pltpu.make_async_remote_copy(
        src_ref=schur,
        dst_ref=matrix.at[half],
        send_sem=matrix_sem.at[1],
        recv_sem=matrix_sem.at[2],
        device_id={"rhs": 1 - half},
        device_id_type=MESH,
    )
    send_all(1, lambda peer: common, common_in)
    swap.start()

    def tile(index):
        s, k = index // blocks, lax.rem(index, blocks)
        return s, k, pl.ds(pl.multiple_of(k * FW, FW), FW)

    def product(index, vector):
        s, k, _ = tile(index)
        part = pl.ds(pl.multiple_of(lax.rem(k, half_blocks) * FW, FW), FW)
        return jnp.dot(
            matrix[k // half_blocks, s, part, :], vector[s], preferred_element_type=jnp.float32
        )

    zero = jnp.zeros((8, out.shape[2]), jnp.float32)
    tiles = SUB_DEV * blocks

    def face_copy(turn, k):
        bit = 1 << k
        peer = me + bit - 2 * bit * lax.rem(me // bit, 2)
        return pltpu.make_async_remote_copy(
            src_ref=rounded.at[turn, :, pl.ds(k * FW, FW), :],
            dst_ref=faces.at[turn, k],
            send_sem=face_send.at[turn, k],
            recv_sem=face_recv.at[turn, k],
            device_id={"sub": peer},
            device_id_type=MESH,
        )

    def pick(source, target):
        for s in range(SUB_DEV):
            for i in range(per_sub):
                target[pl.ds(s * per_sub + i, 1), :] = source[s, pl.ds(corner_row[s, i], 1), :]

    def solve_corners(picked):
        solved = jnp.dot(mix[...], picked, precision=EXACT, preferred_element_type=jnp.float32)
        high = solved.astype(jnp.bfloat16).astype(jnp.float32)
        rest = solved - high
        middle = rest.astype(jnp.bfloat16).astype(jnp.float32)
        low = rest - middle
        for s in range(SUB_DEV):
            at = slice(s * per_sub, (s + 1) * per_sub)
            stack = [high[at], middle[at], low[at], jnp.zeros_like(low[at])]
            corner[s] = jnp.concatenate(stack, axis=0).astype(jnp.bfloat16)

    def corner_tile(s, at):
        return jnp.dot(spread[s, at, :], corner[s], preferred_element_type=jnp.float32)

    wait_all(recv_sem, 0, loads_in)
    load_sum = jnp.sum(loads_in[...], axis=0)

    def start_tile(index, carry):
        s, _, at = tile(index)
        force = gravity[s, at, :] + jnp.dot(
            interp[s, at, :], load_sum, precision=EXACT, preferred_element_type=jnp.float32
        )
        res[s, at, :] = force
        weighted[s, at, :] = (weight[s, at, :] * force).astype(jnp.bfloat16)
        return carry

    lax.fori_loop(0, tiles, start_tile, 0)
    pick(res, picks_out)
    send_all(2, lambda peer: picks_out, picks_in)

    wait_all(recv_sem, 1, common_in)
    lanes = common.shape[1]
    per_device = coarse_rows // chunks
    lane = lax.broadcasted_iota(jnp.int32, (1, lanes), 1).astype(jnp.float32)

    def one_hot(names, chunk):
        return jnp.where(names == lane + float(chunk * lanes), 1.0, 0.0).astype(jnp.float32)

    own = jnp.concatenate([one_hot(common[:corners], c) for c in range(chunks)], axis=1)
    names = common_in[:, :corners, :].reshape(n * corners, lanes)
    total = jnp.zeros((corners, n * corners), jnp.float32)
    for c in range(chunks):
        first = corners + c * per_device
        columns = common_in[:, first : first + per_device, :].reshape(n * per_device, lanes)
        left = jnp.dot(own, columns, precision=EXACT, preferred_element_type=jnp.float32)
        total += lax.dot_general(
            left,
            one_hot(names, c),
            (((1,), (1,)), ((), ())),
            precision=EXACT,
            preferred_element_type=jnp.float32,
        )
    mix[...] = total

    local.wait()
    swap.wait()

    def first_tile(index, carry):
        s, _, at = tile(index)
        dirn[s, at, :] = weight[s, at, :] * product(index, weighted)
        return carry

    lax.fori_loop(0, tiles, first_tile, 0)
    wait_all(recv_sem, 2, picks_in)
    picked = picks_in[...].reshape(n * corners, lanes)
    solve_corners(picked)

    acc = zero
    for k in reversed(range(FACES)):
        at = pl.ds(k * FW, FW)
        for s in range(SUB_DEV):
            value = dirn[s, at, :] + corner_tile(s, at)
            dirn[s, at, :] = value
            rounded[0, s, at, :] = value.astype(jnp.bfloat16)
            acc += fold(value * res[s, at, :])
        face_copy(0, k).start()
    own_dot = jnp.sum(acc, axis=0, keepdims=True)

    def apply(turn):
        def body(index, carry):
            s, _, at = tile(index)
            near = rounded[turn, s, at, :].astype(jnp.float32)
            app[s, at, :] = product(index, rounded.at[turn]) + COUPLING * near
            return carry

        lax.fori_loop(0, tiles, body, 0)
        acc = zero
        for k in range(FACES):
            face_copy(turn, k).wait_recv()
            at = pl.ds(k * FW, FW)
            for s in range(SUB_DEV):
                far = jnp.where(slots[k, s] == 0, faces[turn, k, 0], faces[turn, k, 1])
                far = far.astype(jnp.float32)
                value = app[s, at, :] - COUPLING * far
                if turn == 0:
                    app[s, at, :] = value
                acc += fold(value * dirn[s, at, :])
        return acc

    curvature = jnp.sum(apply(0), axis=0, keepdims=True)
    pick(app, sums_out)
    row = lax.broadcasted_iota(jnp.int32, (8, lanes), 0)
    sums_out[pl.ds(corners, 8), :] = jnp.where(
        row == 0, own_dot, jnp.where(row == 1, curvature, 0.0)
    )
    send_all(3, lambda peer: sums_out, sums_in)
    wait_all(recv_sem, 3, sums_in)
    sums = jnp.sum(sums_in[:, corners:, :], axis=0)
    precond_dot = sums[0:1]
    step = precond_dot / sums[1:2]
    solve_corners(picked - step * sums_in[:, :corners, :].reshape(n * corners, lanes))

    def update_tile(index, carry):
        s, _, at = tile(index)
        value = res[s, at, :] - step * app[s, at, :]
        res[s, at, :] = value
        weighted[s, at, :] = (weight[s, at, :] * value).astype(jnp.bfloat16)
        return carry

    lax.fori_loop(0, tiles, update_tile, 0)

    def second_tile(index, acc):
        s, _, at = tile(index)
        value = weight[s, at, :] * product(index, weighted) + corner_tile(s, at)
        app[s, at, :] = value
        return acc + fold(value * res[s, at, :])

    dots_out[0] = lax.fori_loop(0, tiles, second_tile, zero)
    send_all(4, lambda peer: dots_out.at[0], dots_in.at[0])
    out[...] = step[None] * dirn[...]
    wait_all(recv_sem, 4, dots_in.at[0])
    next_dot = jnp.sum(jnp.sum(dots_in[0], axis=0), axis=0, keepdims=True)
    ratio = next_dot / precond_dot
    for k in reversed(range(FACES)):
        at = pl.ds(k * FW, FW)
        for s in range(SUB_DEV):
            value = app[s, at, :] + ratio * dirn[s, at, :]
            dirn[s, at, :] = value
            rounded[1, s, at, :] = value.astype(jnp.bfloat16)
        face_copy(1, k).start()
    dots_out[1] = apply(1)
    send_all(5, lambda peer: dots_out.at[1], dots_in.at[1])
    wait_all(recv_sem, 5, dots_in.at[1])
    step = next_dot / jnp.sum(jnp.sum(dots_in[1], axis=0), axis=0, keepdims=True)
    out[...] = out[...] + step[None] * dirn[...]

    for turn in range(2):
        for k in range(FACES):
            face_copy(turn, k).wait_send()
    landed = [loads_in, common_in, picks_in, sums_in, dots_in.at[0], dots_in.at[1]]
    for which, target in enumerate(landed):
        wait_all(send_sem, which, target)


def on_device(
    schur_block,
    scaling,
    gravity_load,
    pressure,
    block_target,
    aero_interp,
    partner_slot,
    corner_row,
    corner_coarse,
    coarse_inverse,
):
    n = lax.axis_size("sub")
    columns = gravity_load.shape[2]
    count, points, _ = pressure.shape
    size = gravity_load.shape[1]
    corners = corner_row.size
    key = (block_target * points + jnp.arange(points)[None, :]).reshape(-1)
    chosen = jnp.arange(SUB_DEV * n * points)[:, None] == key[None, :]
    loads = jnp.dot(
        chosen.astype(jnp.bfloat16),
        pressure.reshape(count * points, columns),
        preferred_element_type=jnp.float32,
    ).reshape(n, SUB_DEV * points, columns)
    names = jnp.broadcast_to(
        corner_coarse.reshape(corners, 1).astype(jnp.float32), (corners, columns)
    )
    inverse = coarse_inverse.reshape(coarse_inverse.shape[0], -1, columns)
    inverse = jnp.swapaxes(inverse, 0, 1).reshape(-1, columns)
    common = jnp.concatenate([names, inverse], axis=0)
    interp = (
        jnp.eye(SUB_DEV, dtype=jnp.float32)[:, None, :, None] * aero_interp.T[None, :, None, :]
    ).reshape(SUB_DEV, size, SUB_DEV * points)
    spread = (corner_row[:, None, :] == jnp.arange(size)[None, :, None]).astype(jnp.bfloat16)
    spread = jnp.concatenate([spread] * 3 + [jnp.zeros_like(spread)], axis=2)
    weight = jnp.broadcast_to(scaling[:, :, None], gravity_load.shape)
    per_sub = corner_row.shape[1]
    vmem = pl.BlockSpec(memory_space=pltpu.VMEM)
    smem = pl.BlockSpec(memory_space=pltpu.SMEM)
    f32, bf16 = jnp.float32, jnp.bfloat16
    field = (SUB_DEV, size, columns)
    return pl.pallas_call(
        functools.partial(kernel, n, coarse_inverse.shape[1] // columns),
        out_shape=jax.ShapeDtypeStruct(field, f32),
        in_specs=[pl.BlockSpec(memory_space=pl.ANY)] + [vmem] * 6 + [smem] * 2,
        out_specs=vmem,
        scratch_shapes=[
            pltpu.VMEM((2,) + schur_block.shape, bf16),
            pltpu.VMEM(field, f32),
            pltpu.VMEM(field, f32),
            pltpu.VMEM(field, f32),
            pltpu.VMEM(field, bf16),
            pltpu.VMEM((2,) + field, bf16),
            pltpu.VMEM((SUB_DEV, 4 * per_sub, columns), bf16),
            pltpu.VMEM((corners, n * corners), f32),
            pltpu.VMEM((2, FACES, SUB_DEV, FW, columns), bf16),
            pltpu.VMEM((corners, columns), f32),
            pltpu.VMEM((corners + 8, columns), f32),
            pltpu.VMEM((2, 8, columns), f32),
            pltpu.VMEM(loads.shape, f32),
            pltpu.VMEM((n,) + common.shape, f32),
            pltpu.VMEM((n, corners, columns), f32),
            pltpu.VMEM((n, corners + 8, columns), f32),
            pltpu.VMEM((2, n, 8, columns), f32),
            pltpu.SemaphoreType.DMA((3,)),
            pltpu.SemaphoreType.DMA((2, FACES)),
            pltpu.SemaphoreType.DMA((2, FACES)),
            pltpu.SemaphoreType.DMA((6,)),
            pltpu.SemaphoreType.DMA((6,)),
        ],
        compiler_params=pltpu.CompilerParams(
            collective_id=0, has_side_effects=True, vmem_limit_bytes=44 << 20
        ),
    )(schur_block, weight, gravity_load, loads, common, interp, spread, partner_slot, corner_row)


def solution(mesh):
    return jax.shard_map(
        on_device,
        mesh=mesh,
        in_specs=(
            P("sub", "rhs", None),
            P("sub", None),
            P("sub", None, "rhs"),
            P("sub", None, "rhs"),
            P("sub", None),
            P(),
            P(None, "sub"),
            P("sub", None),
            P("sub", None),
            P("sub", None),
        ),
        out_specs=P("sub", None, "rhs"),
        check_vma=False,
    )
```

```python
import functools

import jax
import jax.numpy as jnp
from jax import lax
from jax.experimental import pallas as pl
from jax.experimental.pallas import tpu as pltpu
from jax.sharding import PartitionSpec as P

SUB_DEV = 2
FACES = 4
FW = 256
COUPLING = 2.0

MESH = pl.DeviceIdType.MESH
EXACT = lax.Precision.HIGHEST


def fold(value):
    return jnp.sum(value.reshape(-1, 8, value.shape[-1]), axis=0)


def kernel(
    n,
    chunks,
    schur,
    scaling,
    gravity,
    pressure,
    key,
    inverse,
    interp,
    slots,
    corner_row,
    corner_coarse,
    out,
    weight,
    loads,
    common,
    matrix,
    res,
    dirn,
    app,
    weighted,
    rounded,
    corner,
    mix,
    faces,
    picks_out,
    sums_out,
    dots_out,
    loads_in,
    common_in,
    picks_in,
    sums_in,
    dots_in,
    matrix_sem,
    face_send,
    face_recv,
    send_sem,
    recv_sem,
):
    me = lax.axis_index("sub")
    half = lax.axis_index("rhs")
    rows = schur.shape[1]
    corners = corner_row.shape[0] * corner_row.shape[1]
    per_sub = corner_row.shape[1]
    halves = gravity.shape[1] // rows
    lanes = common.shape[1]

    local = pltpu.make_async_copy(schur, matrix.at[half], matrix_sem.at[0])
    local.start()

    barrier = pltpu.get_barrier_semaphore()

    def greet(step, carry):
        pl.semaphore_signal(
            barrier, inc=1, device_id={"sub": lax.rem(me + step, n)}, device_id_type=MESH
        )
        return carry

    lax.fori_loop(1, n, greet, 0)
    pl.semaphore_signal(barrier, inc=1, device_id={"rhs": 1 - half}, device_id_type=MESH)

    for s in range(SUB_DEV):
        for k in range(FACES):
            at = slice(k * FW, (k + 1) * FW)
            weight[s, at, :] = jnp.broadcast_to(scaling[s : s + 1, at], (lanes, FW)).T
        for i in range(per_sub):
            name = corner_coarse[s, i].astype(jnp.float32)
            common[pl.ds(s * per_sub + i, 1), :] = jnp.full((1, lanes), name, jnp.float32)
    per_device = inverse.shape[0]
    for c in range(chunks):
        common[pl.ds(corners + c * per_device, per_device), :] = inverse[
            :, c * lanes : (c + 1) * lanes
        ]
    width = loads.shape[1]
    group = 128 // width

    def sum_loads(index, carry):
        row = index * 128 + lax.broadcasted_iota(jnp.int32, (128, key.shape[1]), 0)
        chosen = jnp.where(row == key[...], 1.0, 0.0).astype(jnp.bfloat16)
        total = jnp.dot(chosen, pressure[...], preferred_element_type=jnp.float32)
        loads[pl.ds(index * group, group)] = total.reshape(group, width, lanes)
        return carry

    lax.fori_loop(0, n // group, sum_loads, 0)
    pl.semaphore_wait(barrier, n)

    def send_all(which, source, target):
        def send(step, carry):
            peer = lax.rem(me + step, n)
            pltpu.make_async_remote_copy(
                src_ref=source(peer),
                dst_ref=target.at[me],
                send_sem=send_sem.at[which],
                recv_sem=recv_sem.at[which],
                device_id={"sub": peer},
                device_id_type=MESH,
            ).start()
            return carry

        lax.fori_loop(1, n, send, 0)
        target[me] = source(me)[...]

    def wait_all(sems, which, target):
        view = target.at[pl.ds(0, n - 1)]
        pltpu.make_async_copy(view, view, sems.at[which]).wait()

    send_all(0, lambda peer: loads.at[peer], loads_in)
    swap = pltpu.make_async_remote_copy(
        src_ref=schur,
        dst_ref=matrix.at[half],
        send_sem=matrix_sem.at[1],
        recv_sem=matrix_sem.at[2],
        device_id={"rhs": 1 - half},
        device_id_type=MESH,
    )
    send_all(1, lambda peer: common, common_in)
    swap.start()

    def tile(index):
        s, part = index // halves, lax.rem(index, halves)
        return s, part, pl.ds(pl.multiple_of(part * rows, rows), rows)

    def product(index, vector):
        s, part, _ = tile(index)
        return jnp.dot(matrix[part, s], vector[s], preferred_element_type=jnp.float32)

    zero = jnp.zeros((8, out.shape[2]), jnp.float32)
    tiles = SUB_DEV * halves

    def face_copy(turn, k):
        bit = 1 << k
        peer = me + bit - 2 * bit * lax.rem(me // bit, 2)
        return pltpu.make_async_remote_copy(
            src_ref=rounded.at[turn, :, pl.ds(k * FW, FW), :],
            dst_ref=faces.at[turn, k],
            send_sem=face_send.at[turn, k],
            recv_sem=face_recv.at[turn, k],
            device_id={"sub": peer},
            device_id_type=MESH,
        )

    def pick(source, target):
        for s in range(SUB_DEV):
            for i in range(per_sub):
                target[pl.ds(s * per_sub + i, 1), :] = source[s, pl.ds(corner_row[s, i], 1), :]

    def solve_corners(picked):
        solved = jnp.dot(mix[...], picked, precision=EXACT, preferred_element_type=jnp.float32)
        high = solved.astype(jnp.bfloat16).astype(jnp.float32)
        rest = solved - high
        middle = rest.astype(jnp.bfloat16).astype(jnp.float32)
        low = rest - middle
        for s in range(SUB_DEV):
            at = slice(s * per_sub, (s + 1) * per_sub)
            stack = [high[at], middle[at], low[at], jnp.zeros_like(low[at])]
            corner[s] = jnp.concatenate(stack, axis=0).astype(jnp.bfloat16)

    places = []
    column = lax.broadcasted_iota(jnp.int32, (1, 4 * per_sub), 1)
    for s in range(SUB_DEV):
        place = jnp.full_like(column, -1)
        for i in range(per_sub):
            mine = (lax.rem(column, per_sub) == i) & (column < 3 * per_sub)
            place = jnp.where(mine, corner_row[s, i], place)
        places.append(place)

    def corner_tile(s, first, size):
        row = first + lax.broadcasted_iota(jnp.int32, (size, 4 * per_sub), 0)
        place = places[s] if isinstance(s, int) else jnp.where(s == 0, places[0], places[1])
        spread = jnp.where(row == place, 1.0, 0.0).astype(jnp.bfloat16)
        return jnp.dot(spread, corner[s], preferred_element_type=jnp.float32)

    wait_all(recv_sem, 0, loads_in)
    load_sum = jnp.sum(loads_in[...], axis=0)

    def start_tile(index, carry):
        s, _, at = tile(index)
        mine = jnp.where(s == 0, load_sum[: width // 2], load_sum[width // 2 :])
        force = gravity[s, at, :] + lax.dot_general(
            interp[:, at],
            mine,
            (((0,), (0,)), ((), ())),
            precision=EXACT,
            preferred_element_type=jnp.float32,
        )
        res[s, at, :] = force
        weighted[s, at, :] = (weight[s, at, :] * force).astype(jnp.bfloat16)
        return carry

    lax.fori_loop(0, tiles, start_tile, 0)
    pick(res, picks_out)
    send_all(2, lambda peer: picks_out, picks_in)

    wait_all(recv_sem, 1, common_in)
    lane = lax.broadcasted_iota(jnp.int32, (1, lanes), 1).astype(jnp.float32)

    def one_hot(names, chunk):
        return jnp.where(names == lane + float(chunk * lanes), 1.0, 0.0).astype(jnp.float32)

    own = jnp.concatenate([one_hot(common[:corners], c) for c in range(chunks)], axis=1)
    names = common_in[:, :corners, :].reshape(n * corners, lanes)
    total = jnp.zeros((corners, n * corners), jnp.float32)
    for c in range(chunks):
        first = corners + c * per_device
        columns = common_in[:, first : first + per_device, :].reshape(n * per_device, lanes)
        left = jnp.dot(own, columns, precision=EXACT, preferred_element_type=jnp.float32)
        total += lax.dot_general(
            left,
            one_hot(names, c),
            (((1,), (1,)), ((), ())),
            precision=EXACT,
            preferred_element_type=jnp.float32,
        )
    mix[...] = total

    local.wait()
    swap.wait()

    def first_tile(index, carry):
        s, _, at = tile(index)
        dirn[s, at, :] = weight[s, at, :] * product(index, weighted)
        return carry

    lax.fori_loop(0, tiles, first_tile, 0)
    wait_all(recv_sem, 2, picks_in)
    picked = picks_in[...].reshape(n * corners, lanes)
    solve_corners(picked)

    acc = zero
    for k in reversed(range(FACES)):
        at = pl.ds(k * FW, FW)
        for s in range(SUB_DEV):
            value = dirn[s, at, :] + corner_tile(s, k * FW, FW)
            dirn[s, at, :] = value
            rounded[0, s, at, :] = value.astype(jnp.bfloat16)
            acc += fold(value * res[s, at, :])
        face_copy(0, k).start()
    own_dot = jnp.sum(acc, axis=0, keepdims=True)

    def apply(turn):
        def body(index, carry):
            s, _, at = tile(index)
            near = rounded[turn, s, at, :].astype(jnp.float32)
            app[s, at, :] = product(index, rounded.at[turn]) + COUPLING * near
            return carry

        lax.fori_loop(0, tiles, body, 0)
        acc = zero
        for k in range(FACES):
            face_copy(turn, k).wait_recv()
            at = pl.ds(k * FW, FW)
            for s in range(SUB_DEV):
                far = jnp.where(slots[s, k] == 0, faces[turn, k, 0], faces[turn, k, 1])
                far = far.astype(jnp.float32)
                value = app[s, at, :] - COUPLING * far
                if turn == 0:
                    app[s, at, :] = value
                acc += fold(value * dirn[s, at, :])
        return acc

    curvature = jnp.sum(apply(0), axis=0, keepdims=True)
    pick(app, sums_out)
    row = lax.broadcasted_iota(jnp.int32, (8, lanes), 0)
    sums_out[pl.ds(corners, 8), :] = jnp.where(
        row == 0, own_dot, jnp.where(row == 1, curvature, 0.0)
    )
    send_all(3, lambda peer: sums_out, sums_in)
    wait_all(recv_sem, 3, sums_in)
    sums = jnp.sum(sums_in[:, corners:, :], axis=0)
    precond_dot = sums[0:1]
    step = precond_dot / sums[1:2]
    solve_corners(picked - step * sums_in[:, :corners, :].reshape(n * corners, lanes))

    def update_tile(index, carry):
        s, _, at = tile(index)
        value = res[s, at, :] - step * app[s, at, :]
        res[s, at, :] = value
        weighted[s, at, :] = (weight[s, at, :] * value).astype(jnp.bfloat16)
        return carry

    lax.fori_loop(0, tiles, update_tile, 0)

    def second_tile(index, acc):
        s, part, at = tile(index)
        value = weight[s, at, :] * product(index, weighted) + corner_tile(s, part * rows, rows)
        app[s, at, :] = value
        return acc + fold(value * res[s, at, :])

    dots_out[0] = lax.fori_loop(0, tiles, second_tile, zero)
    send_all(4, lambda peer: dots_out.at[0], dots_in.at[0])
    out[...] = step[None] * dirn[...]
    wait_all(recv_sem, 4, dots_in.at[0])
    next_dot = jnp.sum(jnp.sum(dots_in[0], axis=0), axis=0, keepdims=True)
    ratio = next_dot / precond_dot
    for k in reversed(range(FACES)):
        at = pl.ds(k * FW, FW)
        for s in range(SUB_DEV):
            value = app[s, at, :] + ratio * dirn[s, at, :]
            dirn[s, at, :] = value
            rounded[1, s, at, :] = value.astype(jnp.bfloat16)
        face_copy(1, k).start()
    dots_out[1] = apply(1)
    send_all(5, lambda peer: dots_out.at[1], dots_in.at[1])
    wait_all(recv_sem, 5, dots_in.at[1])
    step = next_dot / jnp.sum(jnp.sum(dots_in[1], axis=0), axis=0, keepdims=True)
    out[...] = out[...] + step[None] * dirn[...]

    for turn in range(2):
        for k in range(FACES):
            face_copy(turn, k).wait_send()
    landed = [loads_in, common_in, picks_in, sums_in, dots_in.at[0], dots_in.at[1]]
    for which, target in enumerate(landed):
        wait_all(send_sem, which, target)


def on_device(
    schur_block,
    scaling,
    gravity_load,
    pressure,
    block_target,
    aero_interp,
    partner_slot,
    corner_row,
    corner_coarse,
    coarse_inverse,
):
    n = lax.axis_size("sub")
    columns = gravity_load.shape[2]
    count, points, _ = pressure.shape
    size = gravity_load.shape[1]
    corners = corner_row.size
    key = (block_target * points + jnp.arange(points)[None, :]).reshape(1, -1)
    per_sub = corner_row.shape[1]
    vmem = pl.BlockSpec(memory_space=pltpu.VMEM)
    smem = pl.BlockSpec(memory_space=pltpu.SMEM)
    f32, bf16 = jnp.float32, jnp.bfloat16
    field = (SUB_DEV, size, columns)
    common = (corners + coarse_inverse.size // columns, columns)
    return pl.pallas_call(
        functools.partial(kernel, n, coarse_inverse.shape[1] // columns),
        out_shape=jax.ShapeDtypeStruct(field, f32),
        in_specs=[pl.BlockSpec(memory_space=pl.ANY)] + [vmem] * 6 + [smem] * 3,
        out_specs=vmem,
        scratch_shapes=[
            pltpu.VMEM(field, f32),
            pltpu.VMEM((n, SUB_DEV * points, columns), f32),
            pltpu.VMEM(common, f32),
            pltpu.VMEM((2,) + schur_block.shape, bf16),
            pltpu.VMEM(field, f32),
            pltpu.VMEM(field, f32),
            pltpu.VMEM(field, f32),
            pltpu.VMEM(field, bf16),
            pltpu.VMEM((2,) + field, bf16),
            pltpu.VMEM((SUB_DEV, 4 * per_sub, columns), bf16),
            pltpu.VMEM((corners, n * corners), f32),
            pltpu.VMEM((2, FACES, SUB_DEV, FW, columns), bf16),
            pltpu.VMEM((corners, columns), f32),
            pltpu.VMEM((corners + 8, columns), f32),
            pltpu.VMEM((2, 8, columns), f32),
            pltpu.VMEM((n, SUB_DEV * points, columns), f32),
            pltpu.VMEM((n,) + common, f32),
            pltpu.VMEM((n, corners, columns), f32),
            pltpu.VMEM((n, corners + 8, columns), f32),
            pltpu.VMEM((2, n, 8, columns), f32),
            pltpu.SemaphoreType.DMA((3,)),
            pltpu.SemaphoreType.DMA((2, FACES)),
            pltpu.SemaphoreType.DMA((2, FACES)),
            pltpu.SemaphoreType.DMA((6,)),
            pltpu.SemaphoreType.DMA((6,)),
        ],
        compiler_params=pltpu.CompilerParams(
            collective_id=0, has_side_effects=True, vmem_limit_bytes=44 << 20
        ),
    )(
        schur_block,
        scaling,
        gravity_load,
        pressure.reshape(count * points, columns),
        key,
        coarse_inverse,
        aero_interp,
        partner_slot.T,
        corner_row,
        corner_coarse,
    )


def solution(mesh):
    return jax.shard_map(
        on_device,
        mesh=mesh,
        in_specs=(
            P("sub", "rhs", None),
            P("sub", None),
            P("sub", None, "rhs"),
            P("sub", None, "rhs"),
            P("sub", None),
            P(),
            P(None, "sub"),
            P("sub", None),
            P("sub", None),
            P("sub", None),
        ),
        out_specs=P("sub", None, "rhs"),
        check_vma=False,
    )
```

```python
import functools

import jax
import jax.numpy as jnp
from jax import lax
from jax.experimental import pallas as pl
from jax.experimental.pallas import tpu as pltpu
from jax.sharding import PartitionSpec as P

SUB_DEV = 2
FACES = 4
FW = 256
COUPLING = 2.0

MESH = pl.DeviceIdType.MESH
EXACT = lax.Precision.HIGHEST


def fold(value):
    return jnp.sum(value.reshape(-1, 8, value.shape[-1]), axis=0)


def kernel(
    n,
    chunks,
    schur,
    scaling_far,
    gravity_far,
    pressure_far,
    key_far,
    inverse_far,
    interp_far,
    indices,
    out,
    scaling,
    pressure,
    key,
    inverse,
    interp,
    load_sem,
    weight,
    loads,
    common,
    matrix,
    res,
    dirn,
    app,
    weighted,
    rounded,
    corner,
    mix,
    faces,
    picks_out,
    sums_out,
    dots_out,
    loads_in,
    common_in,
    picks_in,
    sums_in,
    dots_in,
    matrix_sem,
    face_send,
    face_recv,
    send_sem,
    recv_sem,
):
    me = lax.axis_index("sub")
    half = lax.axis_index("rhs")
    rows = schur.shape[1]
    per_sub = (indices.shape[1] - FACES) // 2
    corners = SUB_DEV * per_sub
    halves = res.shape[1] // rows
    lanes = common.shape[1]

    local = pltpu.make_async_copy(schur, matrix.at[half], matrix_sem.at[0])
    local.start()
    fetches = []
    for source, target in [
        (scaling_far, scaling),
        (inverse_far, inverse),
        (key_far, key),
        (pressure_far, pressure),
        (interp_far, interp),
        (gravity_far, res),
    ]:
        fetches.append(pltpu.make_async_copy(source, target, load_sem.at[len(fetches)]))
        fetches[-1].start()

    barrier = pltpu.get_barrier_semaphore()

    def greet(step, carry):
        pl.semaphore_signal(
            barrier, inc=1, device_id={"sub": lax.rem(me + step, n)}, device_id_type=MESH
        )
        return carry

    lax.fori_loop(1, n, greet, 0)
    pl.semaphore_signal(barrier, inc=1, device_id={"rhs": 1 - half}, device_id_type=MESH)

    for fetch in fetches:
        fetch.wait()
    for s in range(SUB_DEV):
        for k in range(FACES):
            at = slice(k * FW, (k + 1) * FW)
            weight[s, at, :] = jnp.broadcast_to(scaling[s : s + 1, at], (lanes, FW)).T
        for i in range(per_sub):
            name = indices[s, FACES + per_sub + i].astype(jnp.float32)
            common[pl.ds(s * per_sub + i, 1), :] = jnp.full((1, lanes), name, jnp.float32)
    per_device = inverse.shape[0]
    for c in range(chunks):
        common[pl.ds(corners + c * per_device, per_device), :] = inverse[
            :, c * lanes : (c + 1) * lanes
        ]
    width = loads.shape[1]
    group = 128 // width

    def sum_loads(index, carry):
        row = index * 128 + lax.broadcasted_iota(jnp.int32, (128, key.shape[1]), 0)
        chosen = jnp.where(row == key[...], 1.0, 0.0).astype(jnp.bfloat16)
        total = jnp.dot(chosen, pressure[...], preferred_element_type=jnp.float32)
        loads[pl.ds(index * group, group)] = total.reshape(group, width, lanes)
        return carry

    lax.fori_loop(0, n // group, sum_loads, 0)
    pl.semaphore_wait(barrier, n)

    def send_all(which, source, target):
        def send(step, carry):
            peer = lax.rem(me + step, n)
            pltpu.make_async_remote_copy(
                src_ref=source(peer),
                dst_ref=target.at[me],
                send_sem=send_sem.at[which],
                recv_sem=recv_sem.at[which],
                device_id={"sub": peer},
                device_id_type=MESH,
            ).start()
            return carry

        lax.fori_loop(1, n, send, 0)
        target[me] = source(me)[...]

    def wait_all(sems, which, target):
        view = target.at[pl.ds(0, n - 1)]
        pltpu.make_async_copy(view, view, sems.at[which]).wait()

    send_all(0, lambda peer: loads.at[peer], loads_in)
    swap = pltpu.make_async_remote_copy(
        src_ref=schur,
        dst_ref=matrix.at[half],
        send_sem=matrix_sem.at[1],
        recv_sem=matrix_sem.at[2],
        device_id={"rhs": 1 - half},
        device_id_type=MESH,
    )
    send_all(1, lambda peer: common, common_in)
    swap.start()

    def tile(index):
        s, part = index // halves, lax.rem(index, halves)
        return s, part, pl.ds(pl.multiple_of(part * rows, rows), rows)

    def product(index, vector):
        s, part, _ = tile(index)
        return jnp.dot(matrix[part, s], vector[s], preferred_element_type=jnp.float32)

    zero = jnp.zeros((8, out.shape[2]), jnp.float32)
    tiles = SUB_DEV * halves

    def face_copy(turn, k):
        bit = 1 << k
        peer = me + bit - 2 * bit * lax.rem(me // bit, 2)
        return pltpu.make_async_remote_copy(
            src_ref=rounded.at[turn, :, pl.ds(k * FW, FW), :],
            dst_ref=faces.at[turn, k],
            send_sem=face_send.at[turn, k],
            recv_sem=face_recv.at[turn, k],
            device_id={"sub": peer},
            device_id_type=MESH,
        )

    def pick(source, target):
        for s in range(SUB_DEV):
            for i in range(per_sub):
                target[pl.ds(s * per_sub + i, 1), :] = source[s, pl.ds(indices[s, FACES + i], 1), :]

    def solve_corners(picked):
        solved = jnp.dot(mix[...], picked, precision=EXACT, preferred_element_type=jnp.float32)
        high = solved.astype(jnp.bfloat16).astype(jnp.float32)
        rest = solved - high
        middle = rest.astype(jnp.bfloat16).astype(jnp.float32)
        low = rest - middle
        for s in range(SUB_DEV):
            at = slice(s * per_sub, (s + 1) * per_sub)
            stack = [high[at], middle[at], low[at], jnp.zeros_like(low[at])]
            corner[s] = jnp.concatenate(stack, axis=0).astype(jnp.bfloat16)

    places = []
    column = lax.broadcasted_iota(jnp.int32, (1, 4 * per_sub), 1)
    for s in range(SUB_DEV):
        place = jnp.full_like(column, -1)
        for i in range(per_sub):
            mine = (lax.rem(column, per_sub) == i) & (column < 3 * per_sub)
            place = jnp.where(mine, indices[s, FACES + i], place)
        places.append(place)

    def corner_tile(s, first, size):
        row = first + lax.broadcasted_iota(jnp.int32, (size, 4 * per_sub), 0)
        place = places[s] if isinstance(s, int) else jnp.where(s == 0, places[0], places[1])
        spread = jnp.where(row == place, 1.0, 0.0).astype(jnp.bfloat16)
        return jnp.dot(spread, corner[s], preferred_element_type=jnp.float32)

    wait_all(recv_sem, 0, loads_in)
    load_sum = jnp.sum(loads_in[...], axis=0)

    def start_tile(index, carry):
        s, _, at = tile(index)
        mine = jnp.where(s == 0, load_sum[: width // 2], load_sum[width // 2 :])
        force = res[s, at, :] + lax.dot_general(
            interp[:, at],
            mine,
            (((0,), (0,)), ((), ())),
            precision=EXACT,
            preferred_element_type=jnp.float32,
        )
        res[s, at, :] = force
        weighted[s, at, :] = (weight[s, at, :] * force).astype(jnp.bfloat16)
        return carry

    lax.fori_loop(0, tiles, start_tile, 0)
    pick(res, picks_out)
    send_all(2, lambda peer: picks_out, picks_in)

    wait_all(recv_sem, 1, common_in)
    lane = lax.broadcasted_iota(jnp.int32, (1, lanes), 1).astype(jnp.float32)

    def one_hot(names, chunk):
        return jnp.where(names == lane + float(chunk * lanes), 1.0, 0.0).astype(jnp.float32)

    own = jnp.concatenate([one_hot(common[:corners], c) for c in range(chunks)], axis=1)
    names = common_in[:, :corners, :].reshape(n * corners, lanes)
    total = jnp.zeros((corners, n * corners), jnp.float32)
    for c in range(chunks):
        first = corners + c * per_device
        columns = common_in[:, first : first + per_device, :].reshape(n * per_device, lanes)
        left = jnp.dot(own, columns, precision=EXACT, preferred_element_type=jnp.float32)
        total += lax.dot_general(
            left,
            one_hot(names, c),
            (((1,), (1,)), ((), ())),
            precision=EXACT,
            preferred_element_type=jnp.float32,
        )
    mix[...] = total

    local.wait()
    swap.wait()

    def first_tile(index, carry):
        s, _, at = tile(index)
        dirn[s, at, :] = weight[s, at, :] * product(index, weighted)
        return carry

    lax.fori_loop(0, tiles, first_tile, 0)
    wait_all(recv_sem, 2, picks_in)
    picked = picks_in[...].reshape(n * corners, lanes)
    solve_corners(picked)

    acc = zero
    for k in reversed(range(FACES)):
        at = pl.ds(k * FW, FW)
        for s in range(SUB_DEV):
            value = dirn[s, at, :] + corner_tile(s, k * FW, FW)
            dirn[s, at, :] = value
            rounded[0, s, at, :] = value.astype(jnp.bfloat16)
            acc += fold(value * res[s, at, :])
        face_copy(0, k).start()
    own_dot = jnp.sum(acc, axis=0, keepdims=True)

    def apply(turn):
        def body(index, carry):
            s, _, at = tile(index)
            near = rounded[turn, s, at, :].astype(jnp.float32)
            app[s, at, :] = product(index, rounded.at[turn]) + COUPLING * near
            return carry

        lax.fori_loop(0, tiles, body, 0)
        acc = zero
        for k in range(FACES):
            face_copy(turn, k).wait_recv()
            at = pl.ds(k * FW, FW)
            for s in range(SUB_DEV):
                far = jnp.where(indices[s, k] == 0, faces[turn, k, 0], faces[turn, k, 1])
                far = far.astype(jnp.float32)
                value = app[s, at, :] - COUPLING * far
                if turn == 0:
                    app[s, at, :] = value
                acc += fold(value * dirn[s, at, :])
        return acc

    curvature = jnp.sum(apply(0), axis=0, keepdims=True)
    pick(app, sums_out)
    row = lax.broadcasted_iota(jnp.int32, (8, lanes), 0)
    sums_out[pl.ds(corners, 8), :] = jnp.where(
        row == 0, own_dot, jnp.where(row == 1, curvature, 0.0)
    )
    send_all(3, lambda peer: sums_out, sums_in)
    wait_all(recv_sem, 3, sums_in)
    sums = jnp.sum(sums_in[:, corners:, :], axis=0)
    precond_dot = sums[0:1]
    step = precond_dot / sums[1:2]
    solve_corners(picked - step * sums_in[:, :corners, :].reshape(n * corners, lanes))

    def update_tile(index, carry):
        s, _, at = tile(index)
        value = res[s, at, :] - step * app[s, at, :]
        res[s, at, :] = value
        weighted[s, at, :] = (weight[s, at, :] * value).astype(jnp.bfloat16)
        return carry

    lax.fori_loop(0, tiles, update_tile, 0)

    def second_tile(index, acc):
        s, part, at = tile(index)
        value = weight[s, at, :] * product(index, weighted) + corner_tile(s, part * rows, rows)
        app[s, at, :] = value
        return acc + fold(value * res[s, at, :])

    dots_out[0] = lax.fori_loop(0, tiles, second_tile, zero)
    send_all(4, lambda peer: dots_out.at[0], dots_in.at[0])
    out[...] = step[None] * dirn[...]
    wait_all(recv_sem, 4, dots_in.at[0])
    next_dot = jnp.sum(jnp.sum(dots_in[0], axis=0), axis=0, keepdims=True)
    ratio = next_dot / precond_dot
    for k in reversed(range(FACES)):
        at = pl.ds(k * FW, FW)
        for s in range(SUB_DEV):
            value = app[s, at, :] + ratio * dirn[s, at, :]
            dirn[s, at, :] = value
            rounded[1, s, at, :] = value.astype(jnp.bfloat16)
        face_copy(1, k).start()
    dots_out[1] = apply(1)
    send_all(5, lambda peer: dots_out.at[1], dots_in.at[1])
    wait_all(recv_sem, 5, dots_in.at[1])
    step = next_dot / jnp.sum(jnp.sum(dots_in[1], axis=0), axis=0, keepdims=True)
    out[...] = out[...] + step[None] * dirn[...]

    for turn in range(2):
        for k in range(FACES):
            face_copy(turn, k).wait_send()
    landed = [loads_in, common_in, picks_in, sums_in, dots_in.at[0], dots_in.at[1]]
    for which, target in enumerate(landed):
        wait_all(send_sem, which, target)


def on_device(
    schur_block,
    scaling,
    gravity_load,
    pressure,
    block_target,
    aero_interp,
    partner_slot,
    corner_row,
    corner_coarse,
    coarse_inverse,
):
    n = lax.axis_size("sub")
    columns = gravity_load.shape[2]
    count, points, _ = pressure.shape
    size = gravity_load.shape[1]
    corners = corner_row.size
    key = (block_target * points + jnp.arange(points)[None, :]).reshape(1, -1)
    per_sub = corner_row.shape[1]
    vmem = pl.BlockSpec(memory_space=pltpu.VMEM)
    smem = pl.BlockSpec(memory_space=pltpu.SMEM)
    f32, bf16 = jnp.float32, jnp.bfloat16
    field = (SUB_DEV, size, columns)
    common = (corners + coarse_inverse.size // columns, columns)
    return pl.pallas_call(
        functools.partial(kernel, n, coarse_inverse.shape[1] // columns),
        out_shape=jax.ShapeDtypeStruct(field, f32),
        in_specs=[pl.BlockSpec(memory_space=pltpu.HBM)] * 7 + [smem],
        out_specs=vmem,
        scratch_shapes=[
            pltpu.VMEM(scaling.shape, f32),
            pltpu.VMEM((count * points, columns), bf16),
            pltpu.VMEM(key.shape, jnp.int32),
            pltpu.VMEM(coarse_inverse.shape, f32),
            pltpu.VMEM(aero_interp.shape, f32),
            pltpu.SemaphoreType.DMA((6,)),
            pltpu.VMEM(field, f32),
            pltpu.VMEM((n, SUB_DEV * points, columns), f32),
            pltpu.VMEM(common, f32),
            pltpu.VMEM((2,) + schur_block.shape, bf16),
            pltpu.VMEM(field, f32),
            pltpu.VMEM(field, f32),
            pltpu.VMEM(field, f32),
            pltpu.VMEM(field, bf16),
            pltpu.VMEM((2,) + field, bf16),
            pltpu.VMEM((SUB_DEV, 4 * per_sub, columns), bf16),
            pltpu.VMEM((corners, n * corners), f32),
            pltpu.VMEM((2, FACES, SUB_DEV, FW, columns), bf16),
            pltpu.VMEM((corners, columns), f32),
            pltpu.VMEM((corners + 8, columns), f32),
            pltpu.VMEM((2, 8, columns), f32),
            pltpu.VMEM((n, SUB_DEV * points, columns), f32),
            pltpu.VMEM((n,) + common, f32),
            pltpu.VMEM((n, corners, columns), f32),
            pltpu.VMEM((n, corners + 8, columns), f32),
            pltpu.VMEM((2, n, 8, columns), f32),
            pltpu.SemaphoreType.DMA((3,)),
            pltpu.SemaphoreType.DMA((2, FACES)),
            pltpu.SemaphoreType.DMA((2, FACES)),
            pltpu.SemaphoreType.DMA((6,)),
            pltpu.SemaphoreType.DMA((6,)),
        ],
        compiler_params=pltpu.CompilerParams(
            collective_id=0, has_side_effects=True, vmem_limit_bytes=63 << 20
        ),
    )(
        schur_block,
        scaling,
        gravity_load,
        pressure.reshape(count * points, columns),
        key,
        coarse_inverse,
        aero_interp,
        jnp.concatenate([partner_slot.T, corner_row, corner_coarse], axis=1),
    )


def solution(mesh):
    return jax.shard_map(
        on_device,
        mesh=mesh,
        in_specs=(
            P("sub", "rhs", None),
            P("sub", None),
            P("sub", None, "rhs"),
            P("sub", None, "rhs"),
            P("sub", None),
            P(),
            P(None, "sub"),
            P("sub", None),
            P("sub", None),
            P("sub", None),
        ),
        out_specs=P("sub", None, "rhs"),
        check_vma=False,
    )
```
